256 devices in a mesh: row: 16 (over y, z_lo, core), col: 16 (over x, z_hi).
Axes of the slice: x: 4, y: 4, z: 8 (z_hi: 4, z_lo: 2; z = z_hi * 2 + z_lo), core: 2. Of those that a mesh axis runs over, the one named last changes fastest.
Arguments:
- points: float32 [16, 65536], P(None, ('row', 'col')), may hold values from -6 to 6
- inv_length: float32 [16], replicated, may hold values from 0.2 to 0.6
- solution: float32 [16, 65536], P(None, ('row', 'col')), may hold values from -6 to 6
- residual: float32 [16, 65536], P(None, ('row', 'col')), may hold values from -6 to 6
- direction: float32 [16, 65536], P(None, ('row', 'col')), may hold values from -6 to 6
Outputs:
- new_solution: float32 [16, 65536], P(None, ('row', 'col'))
- new_residual: float32 [16, 65536], P(None, ('row', 'col'))
- new_direction: float32 [16, 65536], P(None, ('row', 'col'))
The draws below stay inside these ranges and needn't reach their ends.
All inputs are finite; a program needn't handle non-finite values.
Results may differ from the reference program's by a relative error of at most 0.00013.
Values sent between devices are 32-bit elements; how exact they have to be, the bound alone decides.
A program may use at most 64 MiB of HBM per device.

```python
import math
import jax
import jax.numpy as jnp
from jax import lax

FEAT = 16
PROBES = 16
NPTS = 65536


def block_levels(rng, shape, pieces, smallest, high):
    level = 1.0
    for axis_at, shards_of in pieces:
        steps = jax.random.uniform(jax.random.fold_in(jax.random.fold_in(rng, 6), axis_at), (shards_of,), jnp.float32, smallest / len(pieces), high / len(pieces))
        level = level * jnp.repeat(jnp.exp(steps), shape[axis_at] // shards_of).reshape((-1,) + (1,) * (len(shape) - 1 - axis_at))
    return level


def bell_draw(key, shape, scale, reach, cuts=(), held_as=jnp.bfloat16):
    loudness = block_levels(key, shape, cuts, -0.22, 0.18) if cuts else 1.0
    values = jax.random.normal(key, shape, jnp.float32) * scale * loudness
    return jnp.minimum(jnp.maximum(values, -reach), reach).astype(held_as)


def setup_inputs(seed: int = 0) -> dict:
    splits = jax.random.split(jax.random.key(seed), 6)
    return {
        "points": bell_draw(splits[0], (FEAT, NPTS), 1.0, 6.0, ((1, 256),), jnp.float32),
        "inv_length": jnp.clip(jnp.exp(jax.random.uniform(splits[1], (FEAT,), jnp.float32, math.log(0.2), math.log(0.6))), 0.2, 0.6),
        "solution": bell_draw(splits[2], (PROBES, NPTS), 1.0, 6.0, ((1, 256),), jnp.float32),
        "residual": bell_draw(splits[3], (PROBES, NPTS), 1.0, 6.0, ((1, 256),), jnp.float32),
        "direction": bell_draw(splits[4], (PROBES, NPTS), 1.0, 6.0, ((1, 256),), jnp.float32),
    }


def reference(points, inv_length, solution, residual, direction):
    scaled = points * inv_length[:, None]
    squares = jnp.sum(scaled * scaled, axis=0)
    point_count = scaled.shape[1]
    block_width = math.gcd(point_count, 512)
    nblocks = point_count // block_width
    query_blocks = scaled.reshape(scaled.shape[0], nblocks, block_width).transpose(1, 0, 2)
    query_squares = squares.reshape(nblocks, block_width)

    def one_block(block_args):
        query, query_sq = block_args
        inner_prod = jnp.einsum('fi,fj->ij', query, scaled, precision=lax.Precision.HIGHEST)
        dist = jnp.maximum(query_sq[:, None] + squares[None, :] - 2.0 * inner_prod, 0.0)
        kernel_tile = jnp.exp(-0.5 * dist)
        return jnp.einsum('ij,pj->pi', kernel_tile, direction, precision=lax.Precision.HIGHEST)

    blocks_out = lax.map(one_block, (query_blocks, query_squares))
    kernel_image = blocks_out.transpose(1, 0, 2).reshape(direction.shape[0], point_count)
    old_norm = jnp.sum(residual * residual, axis=1)
    curvature = jnp.sum(direction * kernel_image, axis=1)
    step_size = old_norm / curvature
    new_solution = solution + step_size[:, None] * direction
    new_residual = residual - step_size[:, None] * kernel_image
    new_norm = jnp.sum(new_residual * new_residual, axis=1)
    new_direction = new_residual + (new_norm / old_norm)[:, None] * direction
    return new_solution, new_residual, new_direction
```

```python
import functools
import math

import jax
import jax.numpy as jnp
from jax import lax
from jax.experimental import pallas as pl
from jax.experimental.pallas import tpu as pltpu
from jax.sharding import PartitionSpec as P

MESH = pl.DeviceIdType.MESH
F32 = jnp.float32
BF16 = jnp.bfloat16
F8 = jnp.float8_e4m3fn

FEAT = 16
PROBES = 16
BLOCK = 256
GROUP = 16
PER = 4
CHUNK = PER * BLOCK
CHUNKS = GROUP // PER
DEPTH = 128
TOP = 17.0
DSCALE = 32.0
DZ = (0, 1, 7, 2, 6, 3, 5, 4)


def parts_of(values):
    high = values.astype(BF16).astype(F32)
    rest = values - high
    mid = rest.astype(BF16).astype(F32)
    return high, mid, (rest - mid).astype(BF16).astype(F32)


def features(points, factor, is_key):
    scaled = points * factor
    high, mid, low = parts_of(scaled)
    half = -0.5 * jnp.sum(scaled * scaled, axis=0, keepdims=True)
    if not is_key:
        half = half + TOP
    sq = parts_of(half)
    row = lax.broadcasted_iota(jnp.int32, (FEAT, BLOCK), 0)
    first = 0 if is_key else 3
    extra = jnp.where((row >= 3 - first) & (row < 6 - first), 1.0, 0.0)
    for i, part in enumerate(sq):
        extra = jnp.where(row == first + i, part, extra)
    if is_key:
        rows = [high, high, mid, high, mid, low, extra]
    else:
        rows = [high, mid, high, low, mid, high, extra]
    return jnp.concatenate(rows + [jnp.zeros((FEAT, BLOCK), F32)], axis=0)


def cg_kernel(
    points_hbm, factor_ref, sol_hbm, res_hbm, dir_hbm,
    new_sol_ref, new_res_ref, new_dir_ref,
    own, sol, res, kbuf, qbuf, kf, qf, db, d8, xs, hs, ls, acc_h, acc_l,
    rs_out, rs_in, ar1_out, ar1_in, ar2_out, ar2_in,
    in_sem, k_send, k_recv, f_send, q_send, q_recv, rs_send, rs_recv, a1_send, a1_recv, a2_send, a2_recv,
):
    row, col = lax.axis_index("row"), lax.axis_index("col")
    y, z_lo, core = row // 4, (row // 2) % 2, row % 2
    x, z = col // 4, (col % 4) * 2 + z_lo

    def plane(dx, dy):
        return (lax.rem(y + dy, 4) * 4 + z_lo * 2 + core, lax.rem(x + dx, 4) * 4 + col % 4)

    def pillar(dz, other):
        to_z = lax.rem(z + dz, 8)
        to_core = 1 - core if other else core
        return (y * 4 + (to_z % 2) * 2 + to_core, x * 4 + to_z // 2)

    def remote(src, dst, send, recv, device):
        return pltpu.make_async_remote_copy(
            src_ref=src, dst_ref=dst, send_sem=send, recv_sem=recv, device_id=device, device_id_type=MESH
        )

    loads = [
        pltpu.make_async_copy(points_hbm, own.at[pl.ds(0, FEAT)], in_sem.at[0]),
        pltpu.make_async_copy(dir_hbm, own.at[pl.ds(FEAT, PROBES)], in_sem.at[1]),
        pltpu.make_async_copy(sol_hbm, sol, in_sem.at[2]),
        pltpu.make_async_copy(res_hbm, res, in_sem.at[3]),
    ]
    for load in loads:
        load.start()

    barrier = pltpu.get_barrier_semaphore()
    for s in range(1, GROUP):
        pl.semaphore_signal(barrier, inc=1, device_id=plane(s // 4, s % 4), device_id_type=MESH)
        pl.semaphore_signal(barrier, inc=1, device_id=pillar(s // 2, s % 2), device_id_type=MESH)
    for load in loads:
        load.wait()
    pl.semaphore_wait(barrier, 2 * (GROUP - 1))

    q_copies, k_copies = {}, {}
    k_copies[1] = remote(own, kbuf.at[1], k_send.at[1], k_recv.at[1], pillar(0, 1))
    for i, dz in enumerate(DZ):
        if i:
            k_copies[2 * i] = remote(own, kbuf.at[2 * i], k_send.at[2 * i], k_recv.at[2 * i], pillar(dz, 0))
    for s in range(1, GROUP):
        q_copies[s] = remote(
            own.at[pl.ds(0, FEAT)], qbuf.at[s], q_send.at[s], q_recv.at[s], plane(s // 4, s % 4)
        )
    k_copies[1].start()
    for s in range(1, GROUP):
        q_copies[s].start()
        if s % 2 == 0:
            k_copies[s].start()

    def forward(slot):
        return remote(kbuf.at[slot], kbuf.at[slot + 1], f_send.at[slot], k_recv.at[slot + 1], pillar(0, 1))

    factor = factor_ref[...]

    def prep_key(slot, source):
        kf[slot * BLOCK:(slot + 1) * BLOCK, :] = features(source[0:FEAT], factor, True).T.astype(BF16)
        vec = source[FEAT:FEAT + PROBES]
        high = vec.astype(BF16).astype(F32)
        db[:, slot * BLOCK:(slot + 1) * BLOCK] = jnp.concatenate([high, vec - high], axis=0).astype(BF16)
        wide = vec * DSCALE
        first = wide.astype(F8).astype(F32)
        d8[:, slot * BLOCK:(slot + 1) * BLOCK] = jnp.concatenate([first, wide - first], axis=0).astype(F8)

    def relay_chunk(chunk):
        for slot in range(chunk * PER, (chunk + 1) * PER, 2):
            if slot:
                k_copies[slot].wait_recv()
                forward(slot).start()

    def prep_key_chunk(chunk):
        for slot in range(chunk * PER, (chunk + 1) * PER):
            if slot == 0:
                prep_key(0, own)
                continue
            if slot % 2:
                k_copies[1].wait_recv() if slot == 1 else forward(slot - 1).wait_recv()
            prep_key(slot, kbuf.at[slot])

    def prep_query(slot, source):
        lanes = pl.ds(pl.multiple_of(slot * BLOCK, BLOCK), BLOCK)
        qf[:, lanes] = features(source, factor, False).astype(BF16)

    def prep_query_chunk(chunk):
        def one(i, carry):
            slot = chunk * PER + i
            remote(
                own.at[pl.ds(0, FEAT)], qbuf.at[slot], q_send.at[slot], q_recv.at[slot], plane(0, 0)
            ).wait_recv()
            prep_query(slot, qbuf[slot])
            return carry
        lax.fori_loop(0, PER, one, 0)

    def exponents(q, k, at):
        lanes = pl.ds(pl.multiple_of(q * CHUNK, CHUNK), CHUNK)
        xs[at][...] = jnp.dot(kf[k * CHUNK:(k + 1) * CHUNK, :], qf[:, lanes], preferred_element_type=F32)

    def entries(at):
        value = jnp.exp2(jnp.minimum(xs[at][...], TOP))
        high = value.astype(BF16)
        hs[at][...] = high
        ls[at][...] = (value - high.astype(F32)).astype(F8)

    def products(k, at):
        keys = slice(k * CHUNK, (k + 1) * CHUNK)
        high = jnp.dot(db[:, keys], hs[at][...], preferred_element_type=F32)
        low = jnp.dot(d8[:, keys], ls[at][...], preferred_element_type=F32)
        if k == 0:
            acc_h[...] = high
            acc_l[...] = low
        else:
            acc_h[...] += high
            acc_l[...] += low

    def image_chunk():
        low = (acc_l[0:PROBES] + acc_l[PROBES:2 * PROBES]) * (1.0 / DSCALE)
        return (acc_h[0:PROBES] + acc_h[PROBES:2 * PROBES] + low) * (2.0 ** -TOP)

    def give(slot, device):
        return remote(rs_out.at[slot], rs_in.at[slot], rs_send.at[slot], rs_recv.at[slot], device)

    def send_chunk(q, first):
        image = image_chunk()
        for i in range(PER):
            rs_out[q * PER + i] = image[:, i * BLOCK:(i + 1) * BLOCK]
        for i in range(first, PER):
            slot = q * PER + i
            give(slot, plane(4 - q, (4 - i) % 4)).start()

    relay_chunk(0)
    prep_key_chunk(0)
    prep_query(0, own[0:FEAT])
    for s in range(1, PER):
        q_copies[s].wait_recv()
        prep_query(s, qbuf[s])
    exponents(0, 0, 0)
    relay_chunk(1)
    for k in range(CHUNKS):
        if k + 1 < CHUNKS:
            if k + 2 < CHUNKS:
                relay_chunk(k + 2)
            prep_key_chunk(k + 1)
            exponents(0, k + 1, (k + 1) % 2)
        else:
            prep_query_chunk(1)
            exponents(1, 0, 0)
        entries(k % 2)
        if k:
            products(k - 1, (k - 1) % 2)

    def query_chunk(q, carry):
        exponents(q, 1, 1)
        entries(0)
        products(CHUNKS - 1, (CHUNKS - 1) % 2)

        @pl.when(q == 1)
        def _():
            send_chunk(0, 1)

        @pl.when(q > 1)
        def _():
            send_chunk(q - 1, 0)

        for k in range(1, CHUNKS - 1):
            exponents(q, k + 1, (k + 1) % 2)
            entries(k % 2)
            products(k - 1, (k - 1) % 2)

        @pl.when(q + 1 < CHUNKS)
        def _():
            prep_query_chunk(q + 1)
            exponents(q + 1, 0, 0)

        entries((CHUNKS - 1) % 2)
        products(CHUNKS - 2, (CHUNKS - 2) % 2)
        return carry

    lax.fori_loop(1, CHUNKS, query_chunk, 0)
    products(CHUNKS - 1, (CHUNKS - 1) % 2)
    send_chunk(CHUNKS - 1, 0)

    image = rs_out[0]
    for s in range(1, GROUP):
        give(s, plane(0, 0)).wait_recv()
        image = image + rs_in[s]

    vec, resid = own[FEAT:FEAT + PROBES], res[...]
    lane = lax.broadcasted_iota(jnp.int32, (PROBES, 128), 1)
    sums = jnp.zeros((PROBES, 128), F32)
    for i, (left, right) in enumerate(((resid, resid), (vec, image), (resid, image), (image, image))):
        sums = jnp.where(lane == i, jnp.sum(left * right, axis=1, keepdims=True), sums)

    def all_sum(value, out, into, send, recv, peer):
        out[...] = value
        copies = [
            remote(out, into.at[s], send.at[s], recv.at[s], peer(s)) for s in range(1, GROUP)
        ]
        for copy in copies:
            copy.start()
        for s, copy in enumerate(copies, 1):
            copy.wait_recv()
            value = value + into[s]
        return value, copies

    sums, a1 = all_sum(sums, ar1_out, ar1_in, a1_send, a1_recv, lambda s: plane(s // 4, s % 4))
    sums, a2 = all_sum(sums, ar2_out, ar2_in, a2_send, a2_recv, lambda s: pillar(s // 2, s % 2))

    old_norm, curvature, cross, square = (sums[:, i:i + 1] for i in range(4))
    step = old_norm / curvature
    new_norm = old_norm - 2.0 * step * cross + step * step * square
    new_res = resid - step * image
    new_sol_ref[...] = sol[...] + step * vec
    new_res_ref[...] = new_res
    new_dir_ref[...] = new_res + (new_norm / old_norm) * vec

    for s in range(1, GROUP):
        q_copies[s].wait_send()
        give(s, plane(0, 0)).wait_send()
    for slot, copy in k_copies.items():
        copy.wait_send()
    for slot in range(2, GROUP, 2):
        forward(slot).wait_send()
    for copy in a1 + a2:
        copy.wait_send()


def on_device(points, inv_length, solution_, residual, direction):
    factor = jnp.broadcast_to((inv_length * math.sqrt(math.log2(math.e)))[:, None], (FEAT, BLOCK))
    shape = jax.ShapeDtypeStruct((PROBES, BLOCK), F32)
    vmem, hbm = pl.BlockSpec(memory_space=pltpu.VMEM), pl.BlockSpec(memory_space=pl.ANY)
    dma = pltpu.SemaphoreType.DMA
    return pl.pallas_call(
        lambda *refs: cg_kernel(*refs[:17], refs[17:19], refs[19:21], refs[21:23], *refs[23:]),
        out_shape=(shape, shape, shape),
        in_specs=[hbm, vmem, hbm, hbm, hbm],
        out_specs=(vmem, vmem, vmem),
        scratch_shapes=[
            pltpu.VMEM((FEAT + PROBES, BLOCK), F32),
            pltpu.VMEM((PROBES, BLOCK), F32),
            pltpu.VMEM((PROBES, BLOCK), F32),
            pltpu.VMEM((GROUP, FEAT + PROBES, BLOCK), F32),
            pltpu.VMEM((GROUP, FEAT, BLOCK), F32),
            pltpu.VMEM((GROUP * BLOCK, DEPTH), BF16),
            pltpu.VMEM((DEPTH, GROUP * BLOCK), BF16),
            pltpu.VMEM((2 * PROBES, GROUP * BLOCK), BF16),
            pltpu.VMEM((2 * PROBES, GROUP * BLOCK), F8),
        ]
        + [pltpu.VMEM((CHUNK, CHUNK), F32)] * 2
        + [pltpu.VMEM((CHUNK, CHUNK), BF16)] * 2
        + [pltpu.VMEM((CHUNK, CHUNK), F8)] * 2
        + [
            pltpu.VMEM((2 * PROBES, CHUNK), F32),
            pltpu.VMEM((2 * PROBES, CHUNK), F32),
            pltpu.VMEM((GROUP, PROBES, BLOCK), F32),
            pltpu.VMEM((GROUP, PROBES, BLOCK), F32),
            pltpu.VMEM((PROBES, 128), F32),
            pltpu.VMEM((GROUP, PROBES, 128), F32),
            pltpu.VMEM((PROBES, 128), F32),
            pltpu.VMEM((GROUP, PROBES, 128), F32),
            dma((4,)),
        ]
        + [dma((GROUP,))] * 11,
        compiler_params=pltpu.CompilerParams(
            collective_id=0, has_side_effects=True, vmem_limit_bytes=48 * 2**20
        ),
    )(points, factor, solution_, residual, direction)


def solution(mesh):
    split = P(None, ("row", "col"))
    return jax.shard_map(
        on_device,
        mesh=mesh,
        in_specs=(split, P(), split, split, split),
        out_specs=(split, split, split),
        check_vma=False,
    )
```

```python
import functools
import math

import jax
import jax.numpy as jnp
from jax import lax
from jax.experimental import pallas as pl
from jax.experimental.pallas import tpu as pltpu
from jax.sharding import PartitionSpec as P

MESH = pl.DeviceIdType.MESH
F32 = jnp.float32
BF16 = jnp.bfloat16
F8 = jnp.float8_e4m3fn

FEAT = 16
PROBES = 16
BLOCK = 256
GROUP = 16
KPER = 4
KCHUNK = KPER * BLOCK
KCHUNKS = GROUP // KPER
QPER = 2
QCHUNK = QPER * BLOCK
QCHUNKS = GROUP // QPER
VMEM_LIMIT = 60 * 2**20
DEPTH = 128
TOP = 17.0
DSCALE = 32.0
DZ = (0, 1, 7, 2, 6, 3, 5, 4)


def parts_of(values):
    high = values.astype(BF16).astype(F32)
    rest = values - high
    mid = rest.astype(BF16).astype(F32)
    return high, mid, (rest - mid).astype(BF16).astype(F32)


def features(points, factor, is_key):
    scaled = points * factor
    high, mid, low = parts_of(scaled)
    half = -0.5 * jnp.sum(scaled * scaled, axis=0, keepdims=True)
    if not is_key:
        half = half + TOP
    sq = parts_of(half)
    row = lax.broadcasted_iota(jnp.int32, (FEAT, BLOCK), 0)
    first = 0 if is_key else 3
    extra = jnp.where((row >= 3 - first) & (row < 6 - first), 1.0, 0.0)
    for i, part in enumerate(sq):
        extra = jnp.where(row == first + i, part, extra)
    if is_key:
        rows = [high, high, mid, high, mid, low, extra]
    else:
        rows = [high, mid, high, low, mid, high, extra]
    return jnp.concatenate(rows + [jnp.zeros((FEAT, BLOCK), F32)], axis=0)


def cg_kernel(
    points_hbm, inverse_ref, res_hbm, dir_hbm,
    image_ref, step_ref, ratio_ref,
    own, res, kbuf, qbuf, kf, qf, db, d8, xs, hs, ls, acc,
    rs_out, rs_in, ar1, ar2,
    in_sem, k_send, k_recv, f_send, q_send, q_recv, rs_send, rs_recv, a1_send, a1_recv, a2_send, a2_recv,
):
    row, col = lax.axis_index("row"), lax.axis_index("col")
    y, z_lo, core = row // 4, (row // 2) % 2, row % 2
    x, z = col // 4, (col % 4) * 2 + z_lo

    def plane(dx, dy):
        return (lax.rem(y + dy, 4) * 4 + z_lo * 2 + core, lax.rem(x + dx, 4) * 4 + col % 4)

    def pillar(dz, other):
        to_z = lax.rem(z + dz, 8)
        to_core = 1 - core if other else core
        return (y * 4 + (to_z % 2) * 2 + to_core, x * 4 + to_z // 2)

    def remote(src, dst, send, recv, device):
        return pltpu.make_async_remote_copy(
            src_ref=src, dst_ref=dst, send_sem=send, recv_sem=recv, device_id=device, device_id_type=MESH
        )

    loads = [
        pltpu.make_async_copy(points_hbm, own.at[pl.ds(0, FEAT)], in_sem.at[0]),
        pltpu.make_async_copy(dir_hbm, own.at[pl.ds(FEAT, PROBES)], in_sem.at[1]),
        pltpu.make_async_copy(res_hbm, res, in_sem.at[2]),
    ]
    for load in loads:
        load.start()

    barrier = pltpu.get_barrier_semaphore()
    for s in range(1, GROUP):
        pl.semaphore_signal(barrier, inc=1, device_id=plane(s // 4, s % 4), device_id_type=MESH)
        pl.semaphore_signal(barrier, inc=1, device_id=pillar(s // 2, s % 2), device_id_type=MESH)
    for load in loads:
        load.wait()
    pl.semaphore_wait(barrier, 2 * (GROUP - 1))

    q_copies, k_copies = {}, {}
    k_copies[1] = remote(own, kbuf.at[1], k_send.at[1], k_recv.at[1], pillar(0, 1))
    for i, dz in enumerate(DZ):
        if i:
            k_copies[2 * i] = remote(own, kbuf.at[2 * i], k_send.at[2 * i], k_recv.at[2 * i], pillar(dz, 0))
    for s in range(1, GROUP):
        q_copies[s] = remote(
            own.at[pl.ds(0, FEAT)], qbuf.at[s], q_send.at[s], q_recv.at[s], plane(s // 4, s % 4)
        )
    k_copies[1].start()
    k_copies[2].start()
    k_copies[4].start()
    for s in range(1, GROUP):
        q_copies[s].start()
        if s % 2 and 6 <= s + 5 < GROUP:
            k_copies[s + 5].start()

    def forward(slot):
        return remote(kbuf.at[slot], kbuf.at[slot + 1], f_send.at[slot], k_recv.at[slot + 1], pillar(0, 1))

    at_row = lax.broadcasted_iota(jnp.int32, (FEAT, FEAT), 0)
    at_lane = lax.broadcasted_iota(jnp.int32, (FEAT, FEAT), 1)
    factor = jnp.sum(jnp.where(at_row == at_lane, inverse_ref[...], 0.0), axis=1, keepdims=True)
    factor = factor * math.sqrt(math.log2(math.e))

    def prep_key(slot, source):
        kf[slot * BLOCK:(slot + 1) * BLOCK, :] = features(source[0:FEAT], factor, True).T.astype(BF16)
        vec = source[FEAT:FEAT + PROBES]
        high = vec.astype(BF16).astype(F32)
        db[:, slot * BLOCK:(slot + 1) * BLOCK] = jnp.concatenate([high, vec - high], axis=0).astype(BF16)
        wide = vec * DSCALE
        first = wide.astype(F8).astype(F32)
        d8[:, slot * BLOCK:(slot + 1) * BLOCK] = jnp.concatenate([first, wide - first], axis=0).astype(F8)

    def relay_chunk(chunk):
        for slot in range(chunk * KPER, (chunk + 1) * KPER, 2):
            if slot:
                k_copies[slot].wait_recv()
                forward(slot).start()

    def prep_key_chunk(chunk, skip):
        for slot in range(chunk * KPER + skip, (chunk + 1) * KPER):
            if slot % 2:
                k_copies[1].wait_recv() if slot == 1 else forward(slot - 1).wait_recv()
            prep_key(slot, kbuf.at[slot])

    def prep_query(slot, source):
        lanes = pl.ds(pl.multiple_of(slot * BLOCK, BLOCK), BLOCK)
        qf[:, lanes] = features(source, factor, False).astype(BF16)

    def exponents(q, k, at):
        lanes = pl.ds(pl.multiple_of(q * QCHUNK, QCHUNK), QCHUNK)
        xs[at][...] = jnp.dot(kf[k * KCHUNK:(k + 1) * KCHUNK, :], qf[:, lanes], preferred_element_type=F32)

    def entries(at):
        value = jnp.exp2(jnp.minimum(xs[at][...], TOP))
        high = value.astype(BF16)
        hs[at][...] = high
        ls[at][...] = (value - high.astype(F32)).astype(F8)

    def products(k, at):
        keys = slice(k * KCHUNK, (k + 1) * KCHUNK)
        high = jnp.dot(db[:, keys], hs[at][...], preferred_element_type=F32)
        low = jnp.dot(d8[:, keys], ls[at][...], preferred_element_type=F32)
        return high + low * (1.0 / DSCALE)

    def block(q, half):
        k = 2 * half
        exponents(q, k, 0)
        exponents(q, k + 1, 1)
        entries(0)
        first = products(k, 0)
        entries(1)
        return first + products(k + 1, 1)

    def give(slot, device):
        return remote(rs_out.at[slot], rs_in.at[slot], rs_send.at[slot], rs_recv.at[slot], device)

    relay_chunk(0)
    relay_chunk(1)
    prep_key(0, own)
    prep_query(0, own[0:FEAT])
    prep_key_chunk(0, 1)
    for s in range(1, QPER):
        q_copies[s].wait_recv()
        prep_query(s, qbuf[s])
    prep_key_chunk(1, 0)
    acc[0] = block(0, 0)

    def first_half(q, carry):
        for i in range(QPER):
            slot = q * QPER + i
            remote(
                own.at[pl.ds(0, FEAT)], qbuf.at[slot], q_send.at[slot], q_recv.at[slot], plane(0, 0)
            ).wait_recv()
        for i in range(QPER):
            prep_query(q * QPER + i, qbuf[q * QPER + i])

        @pl.when(q == QCHUNKS // 2)
        def _():
            relay_chunk(2)

        @pl.when(q == QCHUNKS - 2)
        def _():
            relay_chunk(3)

        acc[q] = block(q, 0)
        return carry

    lax.fori_loop(1, QCHUNKS, first_half, 0)
    prep_key_chunk(2, 0)
    prep_key_chunk(3, 0)

    def second_half(i, carry):
        q = QCHUNKS - 1 - i
        total = acc[q] + block(q, 1)
        image = (total[0:PROBES] + total[PROBES:2 * PROBES]) * (2.0 ** -TOP)
        for j in range(QPER):
            rs_out[q * QPER + j] = image[:, j * BLOCK:(j + 1) * BLOCK]
        for j in range(QPER):
            slot = q * QPER + j

            @pl.when(slot > 0)
            def _():
                give(slot, plane(4 - slot // 4, 4 - slot % 4)).start()

        return carry

    lax.fori_loop(0, QCHUNKS, second_half, 0)

    image = rs_out[0]
    for s in range(1, GROUP):
        give(s, plane(0, 0)).wait_recv()
        image = image + rs_in[s]

    vec, resid = own[FEAT:FEAT + PROBES], res[...]
    image_ref[...] = image
    terms = [resid * resid, vec * image, resid * image, image * image]
    terms = jnp.concatenate([term[:, :128] + term[:, 128:] for term in terms] * 2, axis=0)
    sums = jnp.sum(terms.T, axis=0, keepdims=True)

    def all_sum(value, into, send, recv, peer):
        into[0:1] = value
        copies = [
            remote(into.at[pl.ds(0, 1)], into.at[pl.ds(s, 1)], send.at[s], recv.at[s], peer(s))
            for s in reversed(range(1, GROUP))
        ]
        for copy in copies:
            copy.start()
        for copy in copies:
            copy.wait_recv()
        return jnp.sum(into[...], axis=0, keepdims=True), copies

    sums, a1 = all_sum(sums, ar1, a1_send, a1_recv, lambda s: plane(s // 4, s % 4))
    sums, a2 = all_sum(sums, ar2, a2_send, a2_recv, lambda s: pillar(s // 2, s % 2))

    columns = jnp.broadcast_to(sums, (BLOCK, 128)).T
    old_norm, curvature, cross, square = (columns[i * PROBES:(i + 1) * PROBES] for i in range(4))
    step = old_norm / curvature
    new_norm = old_norm - 2.0 * step * cross + step * step * square
    step_ref[...] = step
    ratio_ref[...] = new_norm / old_norm

    for s in range(1, GROUP):
        q_copies[s].wait_send()
        give(s, plane(0, 0)).wait_send()
    for slot, copy in k_copies.items():
        copy.wait_send()
    for slot in range(2, GROUP, 2):
        forward(slot).wait_send()
    for copy in a1 + a2:
        copy.wait_send()


def on_device(points, inv_length, solution_, residual, direction):
    vmem, hbm = pl.BlockSpec(memory_space=pltpu.VMEM), pl.BlockSpec(memory_space=pl.ANY)
    dma = pltpu.SemaphoreType.DMA
    image, step, ratio = pl.pallas_call(
        lambda *refs: cg_kernel(*refs[:15], refs[15:17], refs[17:19], refs[19:21], *refs[21:]),
        out_shape=(jax.ShapeDtypeStruct((PROBES, BLOCK), F32),) * 3,
        in_specs=[hbm, vmem, hbm, hbm],
        out_specs=(vmem, vmem, vmem),
        scratch_shapes=[
            pltpu.VMEM((FEAT + PROBES, BLOCK), F32),
            pltpu.VMEM((PROBES, BLOCK), F32),
            pltpu.VMEM((GROUP, FEAT + PROBES, BLOCK), F32),
            pltpu.VMEM((GROUP, FEAT, BLOCK), F32),
            pltpu.VMEM((GROUP * BLOCK, DEPTH), BF16),
            pltpu.VMEM((DEPTH, GROUP * BLOCK), BF16),
            pltpu.VMEM((2 * PROBES, GROUP * BLOCK), BF16),
            pltpu.VMEM((2 * PROBES, GROUP * BLOCK), F8),
        ]
        + [pltpu.VMEM((KCHUNK, QCHUNK), F32)] * 2
        + [pltpu.VMEM((KCHUNK, QCHUNK), BF16)] * 2
        + [pltpu.VMEM((KCHUNK, QCHUNK), F8)] * 2
        + [
            pltpu.VMEM((QCHUNKS, 2 * PROBES, QCHUNK), F32),
            pltpu.VMEM((GROUP, PROBES, BLOCK), F32),
            pltpu.VMEM((GROUP, PROBES, BLOCK), F32),
            pltpu.VMEM((GROUP, 128), F32),
            pltpu.VMEM((GROUP, 128), F32),
            dma((3,)),
        ]
        + [dma((GROUP,))] * 11,
        compiler_params=pltpu.CompilerParams(
            collective_id=0, has_side_effects=True, vmem_limit_bytes=VMEM_LIMIT
        ),
    )(points, inv_length[None, :], residual, direction)
    new_residual = residual - step * image
    return solution_ + step * direction, new_residual, new_residual + ratio * direction


def solution(mesh):
    split = P(None, ("row", "col"))
    return jax.shard_map(
        on_device,
        mesh=mesh,
        in_specs=(split, P(), split, split, split),
        out_specs=(split, split, split),
        check_vma=False,
    )
```

```python
import functools
import math

import jax
import jax.numpy as jnp
from jax import lax
from jax.experimental import pallas as pl
from jax.experimental.pallas import tpu as pltpu
from jax.sharding import PartitionSpec as P

MESH = pl.DeviceIdType.MESH
F32 = jnp.float32
BF16 = jnp.bfloat16
F8 = jnp.float8_e4m3fn

FEAT = 16
PROBES = 16
BLOCK = 256
GROUP = 16
CHIPS = 128
KPER = 4
KCHUNK = KPER * BLOCK
KCHUNKS = GROUP // KPER
QPER = 2
QCHUNK = QPER * BLOCK
QCHUNKS = GROUP // QPER
VMEM_LIMIT = 60 * 2**20
RELAYS_FIRST = ((2, (6,)), (3, (12,)))
RELAYS_SECOND = ((0, (8, 10)), (2, (14,)))
DEPTH = 128
TOP = 17.0
DSCALE = 32.0
KEYS = ((0, 0), (0, 1), (1, 0), (7, 0), (1, 1), (7, 1), (2, 0), (2, 1), (6, 0), (6, 1), (3, 0), (3, 1), (5, 0), (5, 1), (4, 0), (4, 1))
FAR = KEYS.index((4, 0))
RELAYED = {KEYS.index((dz, 0)): KEYS.index((dz, 1)) for dz in range(1, 8)}


def parts_of(values):
    high = values.astype(BF16)
    rest = values - high.astype(F32)
    mid = rest.astype(BF16)
    return high, mid, (rest - mid.astype(F32)).astype(BF16)


def features(points, factor, is_key):
    scaled = points * factor
    high, mid, low = parts_of(scaled)
    half = -0.5 * jnp.sum(scaled * scaled, axis=0, keepdims=True)
    if not is_key:
        half = half + TOP
    row = lax.broadcasted_iota(jnp.int32, (FEAT, BLOCK), 0)
    first = 0 if is_key else 3
    extra = jnp.where((row >= 3 - first) & (row < 6 - first), 1.0, 0.0)
    for i, part in enumerate(parts_of(half)):
        extra = jnp.where(row == first + i, part.astype(F32), extra)
    extra = extra.astype(BF16)
    blank = jnp.zeros((FEAT, BLOCK), BF16)
    if is_key:
        return [high, high, mid, high, mid, low, extra, blank]
    return [high, mid, high, low, mid, high, extra, blank]


def cg_kernel(
    points_hbm, inverse_ref, res_hbm, dir_hbm,
    image_ref, step_ref, ratio_ref,
    own, res, kbuf, qbuf, kf, qf, db, d8, xs, hs, ls, acc,
    rs_out, rs_in, pair, chips,
    in_sem, k_send, k_recv, f_send, q_send, q_recv, rs_send, rs_recv, a1_send, a1_recv, a2_send, a2_recv,
):
    row, col = lax.axis_index("row"), lax.axis_index("col")
    y, z_lo, core = row // 4, (row // 2) % 2, row % 2
    x, z = col // 4, (col % 4) * 2 + z_lo

    def plane(dx, dy):
        return (lax.rem(y + dy, 4) * 4 + z_lo * 2 + core, lax.rem(x + dx, 4) * 4 + col % 4)

    def near(i):
        return i + (i // 2) * (1 - 2 * (i % 2))

    def taker(slot):
        return plane(near(slot // 4), near(slot % 4))

    def owner(slot):
        return plane(4 - near(slot // 4), 4 - near(slot % 4))

    def pillar(dz, other):
        to_z = lax.rem(z + dz, 8)
        to_core = 1 - core if other else core
        return (y * 4 + (to_z % 2) * 2 + to_core, x * 4 + to_z // 2)

    def remote(src, dst, send, recv, device):
        return pltpu.make_async_remote_copy(
            src_ref=src, dst_ref=dst, send_sem=send, recv_sem=recv, device_id=device, device_id_type=MESH
        )

    loads = [
        pltpu.make_async_copy(points_hbm, own.at[pl.ds(0, FEAT)], in_sem.at[0]),
        pltpu.make_async_copy(dir_hbm, own.at[pl.ds(FEAT, PROBES)], in_sem.at[1]),
        pltpu.make_async_copy(res_hbm, res, in_sem.at[2]),
    ]
    barrier = pltpu.get_barrier_semaphore()
    for s in reversed(range(1, GROUP)):
        pl.semaphore_signal(barrier, inc=1, device_id=pillar(*KEYS[s]), device_id_type=MESH)
        pl.semaphore_signal(barrier, inc=1, device_id=taker(s), device_id_type=MESH)
    for load in loads:
        load.start()
    for load in loads:
        load.wait()
    at_row = lax.broadcasted_iota(jnp.int32, (FEAT, FEAT), 0)
    at_lane = lax.broadcasted_iota(jnp.int32, (FEAT, FEAT), 1)
    factor = jnp.sum(jnp.where(at_row == at_lane, inverse_ref[...], 0.0), axis=1, keepdims=True)
    factor = factor * math.sqrt(math.log2(math.e))

    def prep_key(slot, source):
        rows = jnp.concatenate(features(source[0:FEAT], factor, True), axis=0)
        kf[slot * BLOCK:(slot + 1) * BLOCK, :] = rows.T
        vec = source[FEAT:FEAT + PROBES]
        high = vec.astype(BF16).astype(F32)
        db[:, slot * BLOCK:(slot + 1) * BLOCK] = jnp.concatenate([high, vec - high], axis=0).astype(BF16)
        wide = vec * DSCALE
        first = wide.astype(F8).astype(F32)
        d8[:, slot * BLOCK:(slot + 1) * BLOCK] = jnp.concatenate([first, wide - first], axis=0).astype(F8)

    def prep_query(slot, source):
        lanes = pl.ds(pl.multiple_of(slot * BLOCK, BLOCK), BLOCK)
        for i, part in enumerate(features(source, factor, False)):
            qf[i * FEAT:(i + 1) * FEAT, lanes] = part

    prep_key(0, own)
    prep_query(0, own[0:FEAT])
    pl.semaphore_wait(barrier, 2 * (GROUP - 1))

    q_copies, k_copies = {}, {}
    for s in (1, 2, 3, 6, 8, 10, 12):
        k_copies[s] = remote(own, kbuf.at[s], k_send.at[s], k_recv.at[s], pillar(*KEYS[s]))
    for s in range(1, GROUP):
        q_copies[s] = remote(
            own.at[pl.ds(0, FEAT)], qbuf.at[s], q_send.at[s], q_recv.at[s // 4], taker(s)
        )
    for s in range(1, GROUP):
        if s in k_copies:
            k_copies[s].start()
        q_copies[s].start()
    k_copies[FAR] = remote(kbuf.at[FAR - 2], kbuf.at[FAR], k_send.at[FAR], k_recv.at[FAR], pillar(7, 0))

    def forward(slot):
        to = RELAYED[slot]
        return remote(kbuf.at[slot], kbuf.at[to], f_send.at[slot], k_recv.at[to], pillar(0, 1))

    def relay(*slots):
        for slot in slots:
            k_copies[slot].wait_recv()
            forward(slot).start()
            if slot == FAR - 2:
                k_copies[FAR].start()

    def wait_keys(start, stop):
        for slot in range(start, stop):
            if slot == 1:
                k_copies[1].wait_recv()
            elif slot not in RELAYED:
                remote(own, kbuf.at[slot], k_send.at[slot], k_recv.at[slot], pillar(0, 1)).wait_recv()

    def prep_keys(start, stop):
        for slot in range(start, stop):
            prep_key(slot, kbuf.at[slot])

    def wait_queries(group, skip):
        blocks = qbuf.at[pl.ds(group * 4 + skip, 4 - skip)]
        remote(blocks, blocks, q_send.at[0], q_recv.at[group], taker(0)).wait_recv()

    def exponents(q, k, at):
        lanes = pl.ds(pl.multiple_of(q * QCHUNK, QCHUNK), QCHUNK)
        xs[at][...] = jnp.dot(kf[k * KCHUNK:(k + 1) * KCHUNK, :], qf[:, lanes], preferred_element_type=F32)

    def entries(at):
        value = jnp.exp2(jnp.minimum(xs[at][...], TOP))
        high = value.astype(BF16)
        hs[at][...] = high
        ls[at][...] = (value - high.astype(F32)).astype(F8)

    def products(k, at):
        keys = slice(k * KCHUNK, (k + 1) * KCHUNK)
        high = jnp.dot(db[:, keys], hs[at][...], preferred_element_type=F32)
        low = jnp.dot(d8[:, keys], ls[at][...], preferred_element_type=F32)
        return high + low * (1.0 / DSCALE)

    def block(first, second):
        exponents(*first, 0)
        exponents(*second, 1)
        entries(0)
        one = products(first[1], 0)
        entries(1)
        return one, products(second[1], 1)

    def give(slot, device):
        return remote(rs_out.at[slot], rs_in.at[slot], rs_send.at[slot], rs_recv.at[0], device)

    wait_keys(1, 2)
    relay(2, 3)
    wait_queries(0, 1)
    prep_keys(1, 4)
    for s in range(1, 2 * QPER):
        prep_query(s, qbuf[s])
    acc[0], acc[1] = block((0, 0), (1, 0))

    def first_keys(p, carry):
        wait_queries(p, 0)
        for i in range(2 * QPER):
            prep_query(p * 2 * QPER + i, qbuf[p * 2 * QPER + i])

        for at, slots in RELAYS_FIRST:
            pl.when(p == at)(functools.partial(relay, *slots))

        acc[2 * p], acc[2 * p + 1] = block((2 * p, 0), (2 * p + 1, 0))
        return carry

    lax.fori_loop(1, QCHUNKS // 2, first_keys, 0)
    wait_keys(4, 8)
    prep_keys(4, 8)

    def second_keys(p, carry):
        for at, slots in RELAYS_SECOND:
            pl.when(p == at)(functools.partial(relay, *slots))

        one, two = block((2 * p, 1), (2 * p + 1, 1))
        acc[2 * p] += one
        acc[2 * p + 1] += two
        return carry

    lax.fori_loop(0, QCHUNKS // 2, second_keys, 0)
    wait_keys(8, 16)
    prep_keys(8, 16)

    def last_keys(i, carry):
        q = QCHUNKS - 1 - i
        one, two = block((q, 2), (q, 3))
        total = acc[q] + one + two
        image = (total[0:PROBES] + total[PROBES:2 * PROBES]) * (2.0 ** -TOP)
        for j in range(QPER):
            rs_out[q * QPER + j] = image[:, j * BLOCK:(j + 1) * BLOCK]
        for j in range(QPER):
            slot = q * QPER + j

            @pl.when(slot > 0)
            def _():
                give(slot, owner(slot)).start()

        return carry

    lax.fori_loop(0, QCHUNKS, last_keys, 0)

    others = rs_in.at[pl.ds(1, GROUP - 1)]
    remote(others, others, rs_send.at[0], rs_recv.at[0], taker(0)).wait_recv()
    image = rs_out[0] + jnp.sum(rs_in[1:], axis=0)

    vec, resid = own[FEAT:FEAT + PROBES], res[...]
    image_ref[...] = image
    terms = [resid * resid, vec * image, resid * image, image * image]
    terms = jnp.concatenate([term[:, :128] + term[:, 128:] for term in terms] * 2, axis=0)
    sums = jnp.sum(terms.T, axis=0, keepdims=True)

    pair[0:1] = sums
    swap = remote(pair.at[pl.ds(0, 1)], pair.at[pl.ds(1, 1)], a1_send.at[0], a1_recv.at[0], pillar(0, 1))
    swap.start()
    swap.wait_recv()
    chips[0:1] = pair[0:1] + pair[1:2]
    for s in reversed(range(1, CHIPS)):
        dx, dy, dz = near(s // 32), near(s // 8 % 4), (s % 8 + 1) // 2 * (1 if s % 2 else 7)
        to_z = lax.rem(z + dz, 8)
        device = (lax.rem(y + dy, 4) * 4 + to_z % 2 * 2 + core, lax.rem(x + dx, 4) * 4 + to_z // 2)
        remote(chips.at[pl.ds(0, 1)], chips.at[pl.ds(s, 1)], a2_send.at[0], a2_recv.at[0], device).start()
    others = chips.at[pl.ds(1, CHIPS - 1)]
    everyone = remote(others, others, a2_send.at[0], a2_recv.at[0], pillar(0, 1))
    everyone.wait_recv()
    sums = jnp.sum(chips[...], axis=0, keepdims=True)

    columns = jnp.broadcast_to(sums, (BLOCK, 128)).T
    old_norm, curvature, cross, square = (columns[i * PROBES:(i + 1) * PROBES] for i in range(4))
    step = old_norm / curvature
    new_norm = old_norm - 2.0 * step * cross + step * step * square
    step_ref[...] = step
    ratio_ref[...] = new_norm / old_norm

    for s in range(1, GROUP):
        q_copies[s].wait_send()
        give(s, plane(0, 0)).wait_send()
    for slot, copy in k_copies.items():
        copy.wait_send()
    for slot in RELAYED:
        forward(slot).wait_send()
    swap.wait_send()
    everyone.wait_send()


def on_device(points, inv_length, solution_, residual, direction):
    vmem, hbm = pl.BlockSpec(memory_space=pltpu.VMEM), pl.BlockSpec(memory_space=pl.ANY)
    dma = pltpu.SemaphoreType.DMA
    image, step, ratio = pl.pallas_call(
        lambda *refs: cg_kernel(*refs[:15], refs[15:17], refs[17:19], refs[19:21], *refs[21:]),
        out_shape=(jax.ShapeDtypeStruct((PROBES, BLOCK), F32),) * 3,
        in_specs=[hbm, vmem, hbm, hbm],
        out_specs=(vmem, vmem, vmem),
        scratch_shapes=[
            pltpu.VMEM((FEAT + PROBES, BLOCK), F32),
            pltpu.VMEM((PROBES, BLOCK), F32),
            pltpu.VMEM((GROUP, FEAT + PROBES, BLOCK), F32),
            pltpu.VMEM((GROUP, FEAT, BLOCK), F32),
            pltpu.VMEM((GROUP * BLOCK, DEPTH), BF16),
            pltpu.VMEM((DEPTH, GROUP * BLOCK), BF16),
            pltpu.VMEM((2 * PROBES, GROUP * BLOCK), BF16),
            pltpu.VMEM((2 * PROBES, GROUP * BLOCK), F8),
        ]
        + [pltpu.VMEM((KCHUNK, QCHUNK), F32)] * 2
        + [pltpu.VMEM((KCHUNK, QCHUNK), BF16)] * 2
        + [pltpu.VMEM((KCHUNK, QCHUNK), F8)] * 2
        + [
            pltpu.VMEM((QCHUNKS, 2 * PROBES, QCHUNK), F32),
            pltpu.VMEM((GROUP, PROBES, BLOCK), F32),
            pltpu.VMEM((GROUP, PROBES, BLOCK), F32),
            pltpu.VMEM((8, 128), F32),
            pltpu.VMEM((CHIPS, 128), F32),
            dma((3,)),
        ]
        + [dma((GROUP,))] * 11,
        compiler_params=pltpu.CompilerParams(
            collective_id=0, has_side_effects=True, vmem_limit_bytes=VMEM_LIMIT
        ),
    )(points, inv_length[None, :], residual, direction)
    new_residual = residual - step * image
    return solution_ + step * direction, new_residual, new_residual + ratio * direction


def solution(mesh):
    split = P(None, ("row", "col"))
    return jax.shard_map(
        on_device,
        mesh=mesh,
        in_specs=(split, P(), split, split, split),
        out_specs=(split, split, split),
        check_vma=False,
    )
```

```python
import functools
import math

import jax
import jax.numpy as jnp
from jax import lax
from jax.experimental import pallas as pl
from jax.experimental.pallas import tpu as pltpu
from jax.sharding import PartitionSpec as P

MESH = pl.DeviceIdType.MESH
F32 = jnp.float32
BF16 = jnp.bfloat16
F8 = jnp.float8_e4m3fn

FEAT = 16
PROBES = 16
BLOCK = 256
GROUP = 16
CHIPS = 128
KPER = 4
KCHUNK = KPER * BLOCK
KCHUNKS = GROUP // KPER
QPER = 2
QCHUNK = QPER * BLOCK
QCHUNKS = GROUP // QPER
VMEM_LIMIT = 60 * 2**20
RELAYS = ((6,), (12,), (8, 10), (), (14,), ())
DEPTH = 128
TOP = 17.0
DSCALE = 32.0
KEYS = ((0, 0), (0, 1), (1, 0), (7, 0), (1, 1), (7, 1), (2, 0), (2, 1), (6, 0), (6, 1), (3, 0), (3, 1), (5, 0), (5, 1), (4, 0), (4, 1))
PLANE = (
    (0, 0), (0, 1), (0, 3), (1, 0), (3, 0), (1, 1), (1, 3), (3, 1),
    (3, 3), (0, 2), (2, 0), (1, 2), (3, 2), (2, 1), (2, 3), (2, 2),
)
NEAR_PLANE = tuple(range(1, 11))
NEAR_KEYS = (1, 2, 3, 6, 8)
FAR = KEYS.index((4, 0))
RELAYED = {KEYS.index((dz, 0)): KEYS.index((dz, 1)) for dz in range(1, 8)}


def parts_of(values):
    high = values.astype(BF16)
    rest = values - high.astype(F32)
    mid = rest.astype(BF16)
    return high, mid, (rest - mid.astype(F32)).astype(BF16)


def features(points, factor, is_key):
    scaled = points * factor
    high, mid, low = parts_of(scaled)
    half = -0.5 * jnp.sum(scaled * scaled, axis=0, keepdims=True)
    if not is_key:
        half = half + TOP
    row = lax.broadcasted_iota(jnp.int32, (FEAT, BLOCK), 0)
    first = 0 if is_key else 3
    extra = jnp.where((row >= 3 - first) & (row < 6 - first), 1.0, 0.0)
    for i, part in enumerate(parts_of(half)):
        extra = jnp.where(row == first + i, part.astype(F32), extra)
    extra = extra.astype(BF16)
    blank = jnp.zeros((FEAT, BLOCK), BF16)
    if is_key:
        return [high, high, mid, high, mid, low, extra, blank]
    return [high, mid, high, low, mid, high, extra, blank]


def cg_kernel(
    points_hbm, inverse_ref, res_hbm, dir_hbm,
    image_ref, step_ref, ratio_ref,
    own, res, kbuf, qbuf, kf, qf, db, d8, xs, hs, ls, acc,
    rs_out, rs_in, pair, chips,
    in_sem, k_send, k_recv, f_send, q_send, q_recv, rs_send, rs_recv, a1_send, a1_recv, a2_send, a2_recv,
):
    row, col = lax.axis_index("row"), lax.axis_index("col")
    y, z_lo, core = row // 4, (row // 2) % 2, row % 2
    x, z = col // 4, (col % 4) * 2 + z_lo

    def plane(dx, dy):
        return (lax.rem(y + dy, 4) * 4 + z_lo * 2 + core, lax.rem(x + dx, 4) * 4 + col % 4)

    def near(i):
        return i + (i // 2) * (1 - 2 * (i % 2))

    def taker(slot):
        return plane(*PLANE[slot])

    def owner(slot):
        return plane(4 - PLANE[slot][0], 4 - PLANE[slot][1])

    def pillar(dz, other):
        to_z = lax.rem(z + dz, 8)
        to_core = 1 - core if other else core
        return (y * 4 + (to_z % 2) * 2 + to_core, x * 4 + to_z // 2)

    def remote(src, dst, send, recv, device):
        return pltpu.make_async_remote_copy(
            src_ref=src, dst_ref=dst, send_sem=send, recv_sem=recv, device_id=device, device_id_type=MESH
        )

    loads = [
        pltpu.make_async_copy(points_hbm, own.at[pl.ds(0, FEAT)], in_sem.at[0]),
        pltpu.make_async_copy(dir_hbm, own.at[pl.ds(FEAT, PROBES)], in_sem.at[1]),
        pltpu.make_async_copy(res_hbm, res, in_sem.at[2]),
    ]
    barrier = pltpu.get_barrier_semaphore()
    for s in reversed(NEAR_PLANE):
        pl.semaphore_signal(barrier, inc=1, device_id=taker(s), device_id_type=MESH)
    for s in reversed(NEAR_KEYS):
        pl.semaphore_signal(barrier, inc=1, device_id=pillar(*KEYS[s]), device_id_type=MESH)
    for load in loads:
        load.start()
    for load in loads[:2]:
        load.wait()
    at_row = lax.broadcasted_iota(jnp.int32, (FEAT, FEAT), 0)
    at_lane = lax.broadcasted_iota(jnp.int32, (FEAT, FEAT), 1)
    factor = jnp.sum(jnp.where(at_row == at_lane, inverse_ref[...], 0.0), axis=1, keepdims=True)
    factor = factor * math.sqrt(math.log2(math.e))

    def prep_key(slot, source):
        rows = jnp.concatenate(features(source[0:FEAT], factor, True), axis=0)
        kf[slot * BLOCK:(slot + 1) * BLOCK, :] = rows.T
        vec = source[FEAT:FEAT + PROBES]
        high = vec.astype(BF16).astype(F32)
        db[:, slot * BLOCK:(slot + 1) * BLOCK] = jnp.concatenate([high, vec - high], axis=0).astype(BF16)
        wide = vec * DSCALE
        first = wide.astype(F8).astype(F32)
        d8[:, slot * BLOCK:(slot + 1) * BLOCK] = jnp.concatenate([first, wide - first], axis=0).astype(F8)

    def prep_query(slot, source):
        lanes = pl.ds(pl.multiple_of(slot * BLOCK, BLOCK), BLOCK)
        for i, part in enumerate(features(source, factor, False)):
            qf[i * FEAT:(i + 1) * FEAT, lanes] = part

    prep_key(0, own)
    prep_query(0, own[0:FEAT])
    pl.semaphore_wait(barrier, len(NEAR_PLANE) + len(NEAR_KEYS))

    q_copies, k_copies = {}, {}
    for s in (1, 2, 3, 6, 8, 10, 12):
        k_copies[s] = remote(own, kbuf.at[s], k_send.at[s], k_recv.at[s], pillar(*KEYS[s]))
    for s in range(1, GROUP):
        q_copies[s] = remote(
            own.at[pl.ds(0, FEAT)], qbuf.at[s], q_send.at[s], q_recv.at[s // 4], taker(s)
        )
    for s in NEAR_PLANE:
        if s in NEAR_KEYS:
            k_copies[s].start()
        q_copies[s].start()
    k_copies[FAR] = remote(kbuf.at[FAR - 2], kbuf.at[FAR], k_send.at[FAR], k_recv.at[FAR], pillar(7, 0))

    def forward(slot):
        to = RELAYED[slot]
        return remote(kbuf.at[slot], kbuf.at[to], f_send.at[slot], k_recv.at[to], pillar(0, 1))

    def relay(*slots):
        for slot in slots:
            k_copies[slot].wait_recv()
            forward(slot).start()
            if slot == FAR - 2:
                k_copies[FAR].start()

    def wait_keys(start, stop):
        for slot in range(start, stop):
            if slot == 1:
                k_copies[1].wait_recv()
            elif slot not in RELAYED:
                remote(own, kbuf.at[slot], k_send.at[slot], k_recv.at[slot], pillar(0, 1)).wait_recv()

    def prep_keys(start, stop):
        for slot in range(start, stop):
            prep_key(slot, kbuf.at[slot])

    def wait_queries(group, skip):
        blocks = qbuf.at[pl.ds(group * 4 + skip, 4 - skip)]
        remote(blocks, blocks, q_send.at[0], q_recv.at[group], taker(0)).wait_recv()

    def exponents(q, k, at):
        lanes = pl.ds(pl.multiple_of(q * QCHUNK, QCHUNK), QCHUNK)
        xs[at][...] = jnp.dot(kf[k * KCHUNK:(k + 1) * KCHUNK, :], qf[:, lanes], preferred_element_type=F32)

    def entries(at):
        value = jnp.exp2(jnp.minimum(xs[at][...], TOP))
        high = value.astype(BF16)
        hs[at][...] = high
        ls[at][...] = (value - high.astype(F32)).astype(F8)

    def products(k, at):
        keys = slice(k * KCHUNK, (k + 1) * KCHUNK)
        high = jnp.dot(db[:, keys], hs[at][...], preferred_element_type=F32)
        low = jnp.dot(d8[:, keys], ls[at][...], preferred_element_type=F32)
        return high + low * (1.0 / DSCALE)

    def block(first, second):
        exponents(*first, 0)
        exponents(*second, 1)
        entries(0)
        one = products(first[1], 0)
        entries(1)
        return one, products(second[1], 1)

    def give(slot, device):
        return remote(rs_out.at[slot], rs_in.at[slot], rs_send.at[slot], rs_recv.at[0], device)

    wait_keys(1, 2)
    relay(2, 3)
    wait_queries(0, 1)
    for s in (10, 12):
        k_copies[s].start()
    for s in range(11, 15):
        q_copies[s].start()
    prep_keys(1, 4)
    for s in range(1, 2 * QPER):
        prep_query(s, qbuf[s])
    acc[0], acc[1] = block((0, 0), (1, 0))

    def take_queries(p):
        wait_queries(p, 0)
        for i in range(2 * QPER):
            prep_query(p * 2 * QPER + i, qbuf[p * 2 * QPER + i])

    wait_queries(1, 0)
    q_copies[15].start()
    for i in range(2 * QPER, 4 * QPER):
        prep_query(i, qbuf[i])
    acc[2], acc[3] = block((2, 0), (3, 0))
    take_queries(2)
    relay(*RELAYS[0])
    acc[4], acc[5] = block((4, 0), (5, 0))
    wait_keys(4, 8)
    prep_keys(4, 8)

    def second_keys(p, carry):
        for at, slots in enumerate(RELAYS[1:4]):
            pl.when(p == at)(functools.partial(relay, *slots))

        one, two = block((2 * p, 1), (2 * p + 1, 1))
        acc[2 * p] += one
        acc[2 * p + 1] += two
        return carry

    lax.fori_loop(0, QCHUNKS // 2 - 1, second_keys, 0)
    take_queries(3)
    relay(*RELAYS[4])
    for q in (6, 7):
        one, two = block((q, 0), (q, 1))
        acc[q] = one + two
    relay(*RELAYS[5])
    wait_keys(8, 16)
    prep_keys(8, 16)

    def last_keys(i, carry):
        q = QCHUNKS - 1 - i
        one, two = block((q, 2), (q, 3))
        total = acc[q] + one + two
        image = (total[0:PROBES] + total[PROBES:2 * PROBES]) * (2.0 ** -TOP)
        for j in range(QPER):
            rs_out[q * QPER + j] = image[:, j * BLOCK:(j + 1) * BLOCK]
        for chunk in range(QCHUNKS):

            @pl.when(q == chunk)
            def _():
                for slot in range(max(1, chunk * QPER), (chunk + 1) * QPER):
                    give(slot, owner(slot)).start()

        return carry

    lax.fori_loop(0, QCHUNKS, last_keys, 0)

    others = rs_in.at[pl.ds(1, GROUP - 1)]
    remote(others, others, rs_send.at[0], rs_recv.at[0], taker(0)).wait_recv()
    image = rs_out[0] + jnp.sum(rs_in[1:], axis=0)

    loads[2].wait()
    vec, resid = own[FEAT:FEAT + PROBES], res[...]
    image_ref[...] = image
    terms = [resid * resid, vec * image, resid * image, image * image]
    terms = jnp.concatenate([term[:, :128] + term[:, 128:] for term in terms] * 2, axis=0)
    sums = jnp.sum(terms.T, axis=0, keepdims=True)

    pair[0:1] = sums
    swap = remote(pair.at[pl.ds(0, 1)], pair.at[pl.ds(1, 1)], a1_send.at[0], a1_recv.at[0], pillar(0, 1))
    swap.start()
    swap.wait_recv()
    chips[0:1] = pair[0:1] + pair[1:2]
    for s in reversed(range(1, CHIPS)):
        dx, dy, dz = near(s // 32), near(s // 8 % 4), (s % 8 + 1) // 2 * (1 if s % 2 else 7)
        to_z = lax.rem(z + dz, 8)
        device = (lax.rem(y + dy, 4) * 4 + to_z % 2 * 2 + core, lax.rem(x + dx, 4) * 4 + to_z // 2)
        remote(chips.at[pl.ds(0, 1)], chips.at[pl.ds(s, 1)], a2_send.at[0], a2_recv.at[0], device).start()
    others = chips.at[pl.ds(1, CHIPS - 1)]
    everyone = remote(others, others, a2_send.at[0], a2_recv.at[0], pillar(0, 1))
    everyone.wait_recv()
    sums = jnp.sum(chips[...], axis=0, keepdims=True)

    columns = jnp.broadcast_to(sums, (BLOCK, 128)).T
    old_norm, curvature, cross, square = (columns[i * PROBES:(i + 1) * PROBES] for i in range(4))
    step = old_norm / curvature
    new_norm = old_norm - 2.0 * step * cross + step * step * square
    step_ref[...] = step
    ratio_ref[...] = new_norm / old_norm

    for s in range(1, GROUP):
        q_copies[s].wait_send()
        give(s, plane(0, 0)).wait_send()
    for slot, copy in k_copies.items():
        copy.wait_send()
    for slot in RELAYED:
        forward(slot).wait_send()
    swap.wait_send()
    everyone.wait_send()


def on_device(points, inv_length, solution_, residual, direction):
    vmem, hbm = pl.BlockSpec(memory_space=pltpu.VMEM), pl.BlockSpec(memory_space=pl.ANY)
    dma = pltpu.SemaphoreType.DMA
    image, step, ratio = pl.pallas_call(
        lambda *refs: cg_kernel(*refs[:15], refs[15:17], refs[17:19], refs[19:21], *refs[21:]),
        out_shape=(pltpu.VMEM((PROBES, BLOCK), F32),) * 3,
        in_specs=[hbm, vmem, hbm, hbm],
        out_specs=(vmem, vmem, vmem),
        scratch_shapes=[
            pltpu.VMEM((FEAT + PROBES, BLOCK), F32),
            pltpu.VMEM((PROBES, BLOCK), F32),
            pltpu.VMEM((GROUP, FEAT + PROBES, BLOCK), F32),
            pltpu.VMEM((GROUP, FEAT, BLOCK), F32),
            pltpu.VMEM((GROUP * BLOCK, DEPTH), BF16),
            pltpu.VMEM((DEPTH, GROUP * BLOCK), BF16),
            pltpu.VMEM((2 * PROBES, GROUP * BLOCK), BF16),
            pltpu.VMEM((2 * PROBES, GROUP * BLOCK), F8),
        ]
        + [pltpu.VMEM((KCHUNK, QCHUNK), F32)] * 2
        + [pltpu.VMEM((KCHUNK, QCHUNK), BF16)] * 2
        + [pltpu.VMEM((KCHUNK, QCHUNK), F8)] * 2
        + [
            pltpu.VMEM((QCHUNKS, 2 * PROBES, QCHUNK), F32),
            pltpu.VMEM((GROUP, PROBES, BLOCK), F32),
            pltpu.VMEM((GROUP, PROBES, BLOCK), F32),
            pltpu.VMEM((8, 128), F32),
            pltpu.VMEM((CHIPS, 128), F32),
            dma((3,)),
        ]
        + [dma((GROUP,))] * 11,
        compiler_params=pltpu.CompilerParams(
            collective_id=0, has_side_effects=True, vmem_limit_bytes=VMEM_LIMIT
        ),
    )(points, inv_length[None, :], residual, direction)
    new_residual = residual - step * image
    return solution_ + step * direction, new_residual, new_residual + ratio * direction


def solution(mesh):
    split = P(None, ("row", "col"))
    return jax.shard_map(
        on_device,
        mesh=mesh,
        in_specs=(split, P(), split, split, split),
        out_specs=(split, split, split),
        check_vma=False,
    )
```
